32 devices in a mesh: dom: 8 (over z, x), sub: 4 (over y, core).
Axes of the slice: x: 2, y: 2, z: 4, core: 2. Of those that a mesh axis runs over, the one named last changes fastest.
Arguments:
- features: bfloat16 [65536, 512], P(('dom', 'sub')), may hold values from -6 to 6
- hub_features: bfloat16 [512, 512], P(('dom', 'sub')), may hold values from -6 to 6
- w_self: bfloat16 [512, 512], replicated, may hold values from -0.25 to 0.25
- w_neigh: bfloat16 [512, 512], replicated, may hold values from -1 to 1
- out_bias: float32 [512], replicated, may hold values from -3 to 3
- tile_index: int32 [32, 32, 2], P(('dom', 'sub')), may hold values from 0 to 15
- tile_count: int32 [32], P(('dom', 'sub')), may hold values from 1 to 32, as said below
- tile_mask: int32 [1024, 128, 128], P(('dom', 'sub')), may hold values 0 or 1
- mirror_slot: int32 [32, 32, 2], P(('dom', 'sub')), may hold values from -1 to 15, as said below
- mirror_edges: int32 [32, 64, 2048], P(('dom', 'sub')), may hold values 0 or 1
- row_degree: int32 [65536], P(('dom', 'sub')), may hold values from 12 to 40
- hub_degree: int32 [512], P(('dom', 'sub')), may hold values from 32 to 128
- grad_rows: bfloat16 [65536, 512], P(('dom', 'sub')), may hold values from -6 to 6
- grad_hubs: bfloat16 [512, 512], P(('dom', 'sub')), may hold values from -6 to 6
Outputs:
- out_rows: bfloat16 [65536, 512], P(('dom', 'sub'))
- out_hubs: bfloat16 [512, 512], P(('dom', 'sub'))
- d_features: bfloat16 [65536, 512], P(('dom', 'sub'))
- d_hub_features: bfloat16 [512, 512], P(('dom', 'sub'))
- d_w_self: float32 [512, 512], replicated
- d_w_neigh: float32 [512, 512], replicated
- d_bias: float32 [512], replicated
The draws below stay inside these ranges and needn't reach their ends.
Inputs may be any that keep to these rules, and one draw needn't show every extreme that they name: `tile_count`: number of live tile slots of a partition; slots from it on are ignored. Some partition uses all 32. mirror_slot[p, q, c] is an index among master q's 16 hubs, or -1 for an empty slot; the live indices of one (p, q) are distinct; some partition has all 2 slots live from every master. `tile_index`: tile positions may repeat within a partition.
All inputs are finite; a program needn't handle non-finite values. No bound on the sum of `tile_mask` or of `mirror_edges` on one device may be relied on, other than what follows from the above.
Results may differ from the reference program's by a relative error of at most 0.0057.
Values may be sent and summed in bfloat16 or wider, within the bound.
A program may use at most 128 MiB of HBM per device.

```python
import jax
import jax.numpy as jnp
from jax import lax

D = 512
F = 512
ROWS_DEV = 2048
HUB_DEV = 16
CAP = 2
NT = 32
TB = 128
DEVICES = 32


def draw_tile_count(key, part):
    key = jax.random.fold_in(key, 5)
    key_count, key_busy = jax.random.split(key)
    counts = jax.random.randint(key_count, (DEVICES,), max(1, NT // 8), NT // 2 + 1)
    busiest = jax.random.randint(key_busy, (), 0, DEVICES)
    return jnp.where(jnp.arange(DEVICES) == busiest, NT, counts).astype(jnp.int32)


def draw_mirror_slot(key, part):
    key = jax.random.fold_in(key, 11)
    key_count, key_busy, key_perm = jax.random.split(key, 3)
    counts = jax.random.randint(key_count, (DEVICES, DEVICES), 0, CAP + 1)
    busiest = jax.random.randint(key_busy, (), 0, DEVICES)
    counts = jnp.where(jnp.arange(DEVICES)[:, None] == busiest, CAP, counts)
    keys_all = jax.random.split(key_perm, DEVICES * DEVICES)
    chosen = jax.vmap(lambda single: jax.random.permutation(single, HUB_DEV)[:CAP])(keys_all).reshape(DEVICES, DEVICES, CAP)
    return jnp.where(jnp.arange(CAP)[None, None, :] < counts[:, :, None], chosen, -1).astype(jnp.int32)


def plant(values, own_key, least, top_value):
    longest = values.shape.index(max(values.shape))
    spots = []
    for shift in (0, 1):
        where = [jax.random.randint(jax.random.fold_in(own_key, axis), (), 0, length) for axis, length in enumerate(values.shape)]
        where[longest] = (where[longest] + shift) % values.shape[longest]
        spots.append(tuple(where))
    return values.at[spots[0]].set(least).at[spots[1]].set(top_value)


def shard_levels(rng, shape, cuts, low, high):
    level = 1.0
    for dim, parts in cuts:
        steps = jax.random.uniform(jax.random.fold_in(jax.random.fold_in(rng, 6), dim), (parts,), jnp.float32, low / len(cuts), high / len(cuts))
        level = level * jnp.repeat(jnp.exp(steps), shape[dim] // parts).reshape((-1,) + (1,) * (len(shape) - 1 - dim))
    return level


def centred(rng, shape, width, reach, cuts=(), kind=jnp.bfloat16):
    array = width * jax.random.normal(rng, shape, jnp.float32)
    if cuts:
        array = array * shard_levels(rng, shape, cuts, -0.22, 0.18)
    return jnp.clip(array, -reach, reach).astype(kind)


def setup_inputs(seed: int = 0) -> dict:
    streams_of = jax.random.split(jax.random.key(seed), 15)
    return {
        "features": centred(streams_of[0], (DEVICES * ROWS_DEV, D), 1.0, 6.0, ((0, 32),)),
        "hub_features": centred(streams_of[1], (DEVICES * HUB_DEV, D), 1.0, 6.0, ((0, 32),)),
        "w_self": centred(streams_of[2], (D, F), D ** -0.5, 0.25),
        "w_neigh": centred(streams_of[3], (D, F), (D // 16) ** -0.5, 1.0),
        "out_bias": centred(streams_of[4], (F,), 0.5, 3.0, (), jnp.float32),
        "tile_index": plant(jax.random.randint(streams_of[5], (DEVICES, NT, 2), 0, ROWS_DEV // TB), jax.random.fold_in(streams_of[5], 1), 0, (ROWS_DEV // TB) - 1).astype(jnp.int32),
        "tile_count": draw_tile_count(jax.random.fold_in(streams_of[14], 71), 0),
        "tile_mask": plant((jax.random.randint(streams_of[7], (DEVICES * NT, TB, TB), 0, 8) < 1).astype(jnp.int32), jax.random.fold_in(streams_of[7], 1), 0, 1),
        "mirror_slot": draw_mirror_slot(jax.random.fold_in(streams_of[14], 71), 0),
        "mirror_edges": plant((jax.random.randint(streams_of[9], (DEVICES, DEVICES * CAP, ROWS_DEV), 0, 32) < 1).astype(jnp.int32), jax.random.fold_in(streams_of[9], 1), 0, 1),
        "row_degree": plant(jax.random.randint(streams_of[10], (DEVICES * ROWS_DEV,), 12, 41), jax.random.fold_in(streams_of[10], 1), 12, 40).astype(jnp.int32),
        "hub_degree": plant(jax.random.randint(streams_of[11], (DEVICES * HUB_DEV,), 32, 129), jax.random.fold_in(streams_of[11], 1), 32, 128).astype(jnp.int32),
        "grad_rows": centred(streams_of[12], (DEVICES * ROWS_DEV, F), 1.0, 6.0, ((0, 32),)),
        "grad_hubs": centred(streams_of[13], (DEVICES * HUB_DEV, F), 1.0, 6.0, ((0, 32),)),
    }


def silu_slope(values):
    sigma = jax.nn.sigmoid(values)
    return sigma * (1.0 + values * (1.0 - sigma))


def tile_forward(source, tile_pos, live_count, tile_bits):
    n_tiles = source.shape[0] // TB
    live = (jnp.arange(NT) < live_count).astype(jnp.float32)
    weights_tile = tile_bits.astype(jnp.float32) * live[:, None, None]
    picked = source.reshape(n_tiles, TB, -1)[tile_pos[:, 1]].astype(jnp.float32)
    product = jnp.einsum("tij,tjd->tid", weights_tile, picked, precision=lax.Precision.HIGHEST)
    placing = (tile_pos[:, 0][None, :] == jnp.arange(n_tiles)[:, None]).astype(jnp.float32)
    return jnp.einsum("kt,tid->kid", placing, product, precision=lax.Precision.HIGHEST).reshape(source.shape[0], -1)


def tile_backward(source, tile_pos, live_count, tile_bits):
    n_tiles = source.shape[0] // TB
    live = (jnp.arange(NT) < live_count).astype(jnp.float32)
    weights_tile = tile_bits.astype(jnp.float32) * live[:, None, None]
    picked = source.reshape(n_tiles, TB, -1)[tile_pos[:, 0]].astype(jnp.float32)
    product = jnp.einsum("tij,tid->tjd", weights_tile, picked, precision=lax.Precision.HIGHEST)
    placing = (tile_pos[:, 1][None, :] == jnp.arange(n_tiles)[:, None]).astype(jnp.float32)
    return jnp.einsum("kt,tid->kid", placing, product, precision=lax.Precision.HIGHEST).reshape(source.shape[0], -1)


def mirror_info(my_slots, edges):
    live_slot = (my_slots >= 0).reshape(-1)
    owner_row = (jnp.arange(DEVICES, dtype=jnp.int32)[:, None] * HUB_DEV + jnp.maximum(my_slots, 0)).reshape(-1)
    edge_mat = (edges * live_slot[:, None].astype(jnp.int32)).astype(jnp.bfloat16)
    return live_slot, owner_row, edge_mat


def reference(features, hub_features, w_self, w_neigh, out_bias, tile_index, tile_count, tile_mask, mirror_slot, mirror_edges, row_degree, hub_degree, grad_rows, grad_hubs):
    rows_dev = features.reshape(DEVICES, ROWS_DEV, D)
    bits_dev = tile_mask.reshape(DEVICES, NT, TB, TB)
    degree_dev = row_degree.reshape(DEVICES, ROWS_DEV)
    grads_dev = grad_rows.reshape(DEVICES, ROWS_DEV, F)
    zero_half = jnp.zeros((), jnp.bfloat16)

    def mirror_terms(inputs):
        source, my_slots, edges = inputs
        edge_mat = mirror_info(my_slots, edges)[2]
        return jnp.dot(edge_mat, source, preferred_element_type=jnp.float32)

    def settle(partial_value):
        split_parts = partial_value.reshape(DEVICES, DEVICES, CAP, -1)

        def one_master(master):
            selector = (mirror_slot[:, master, :][:, :, None] == jnp.arange(HUB_DEV)[None, None, :]).astype(jnp.float32)
            return jnp.einsum("pch,pcd->hd", selector, split_parts[:, master], precision=lax.Precision.HIGHEST)

        return lax.map(one_master, jnp.arange(DEVICES)).reshape(DEVICES * HUB_DEV, -1)

    mirror_part = lax.map(mirror_terms, (rows_dev, mirror_slot, mirror_edges))
    hub_sum = settle(mirror_part)
    mean_hubs = (hub_sum / hub_degree[:, None].astype(jnp.float32)).astype(jnp.bfloat16)
    pre_hubs = jnp.dot(hub_features, w_self, preferred_element_type=jnp.float32) + jnp.dot(mean_hubs, w_neigh, preferred_element_type=jnp.float32) + out_bias
    out_hubs = jax.nn.silu(pre_hubs).astype(jnp.bfloat16)
    d_pre_hubs = (grad_hubs.astype(jnp.float32) * silu_slope(pre_hubs)).astype(jnp.bfloat16)
    d_sum_hubs = (jnp.dot(d_pre_hubs, w_neigh.T, preferred_element_type=jnp.float32) / hub_degree[:, None].astype(jnp.float32)).astype(jnp.bfloat16)

    init = (jnp.dot(hub_features.T, d_pre_hubs, preferred_element_type=jnp.float32),
            jnp.dot(mean_hubs.T, d_pre_hubs, preferred_element_type=jnp.float32),
            jnp.sum(d_pre_hubs.astype(jnp.float32), axis=0))

    def one_part(totals, inputs):
        source, tile_pos, live_count, tile_bits, my_slots, edges, degree, grads = inputs
        live_slot, owner_row, edge_mat = mirror_info(my_slots, edges)
        degree_col = degree[:, None].astype(jnp.float32)
        mirror_x = jnp.where(live_slot[:, None], hub_features[owner_row], zero_half)
        row_sum = tile_forward(source, tile_pos, live_count, tile_bits) + jnp.dot(edge_mat.T, mirror_x, preferred_element_type=jnp.float32)
        mean_rows = (row_sum / degree_col).astype(jnp.bfloat16)
        pre_rows = jnp.dot(source, w_self, preferred_element_type=jnp.float32) + jnp.dot(mean_rows, w_neigh, preferred_element_type=jnp.float32) + out_bias
        out_part = jax.nn.silu(pre_rows).astype(jnp.bfloat16)
        d_pre = (grads.astype(jnp.float32) * silu_slope(pre_rows)).astype(jnp.bfloat16)
        totals = (totals[0] + jnp.dot(source.T, d_pre, preferred_element_type=jnp.float32),
                  totals[1] + jnp.dot(mean_rows.T, d_pre, preferred_element_type=jnp.float32),
                  totals[2] + jnp.sum(d_pre.astype(jnp.float32), axis=0))
        d_sum_rows = (jnp.dot(d_pre, w_neigh.T, preferred_element_type=jnp.float32) / degree_col).astype(jnp.bfloat16)
        mirror_d = jnp.where(live_slot[:, None], d_sum_hubs[owner_row], zero_half)
        d_part = jnp.dot(d_pre, w_self.T, preferred_element_type=jnp.float32) + tile_backward(d_sum_rows, tile_pos, live_count, tile_bits) + jnp.dot(edge_mat.T, mirror_d, preferred_element_type=jnp.float32)
        mirror_back = jnp.dot(edge_mat, d_sum_rows, preferred_element_type=jnp.float32)
        return totals, (out_part, d_part.astype(jnp.bfloat16), mirror_back)

    totals, (out_parts, d_parts, mirror_back) = lax.scan(one_part, init, (rows_dev, tile_index, tile_count, bits_dev, mirror_slot, mirror_edges, degree_dev, grads_dev))
    d_hub_features = (jnp.dot(d_pre_hubs, w_self.T, preferred_element_type=jnp.float32) + settle(mirror_back)).astype(jnp.bfloat16)
    return (out_parts.reshape(DEVICES * ROWS_DEV, F), out_hubs, d_parts.reshape(DEVICES * ROWS_DEV, D), d_hub_features, totals[0], totals[1], totals[2])
```

```python
import functools

import jax
import jax.numpy as jnp
from jax import lax
from jax.experimental import pallas as pl
from jax.experimental.pallas import tpu as pltpu
from jax.sharding import PartitionSpec as P

MESH = pl.DeviceIdType.MESH


def enter(n, n_sub, me):
    barrier = pltpu.get_barrier_semaphore()

    @pl.loop(1, n)
    def _(k):
        peer = lax.rem(me + k, n)
        pl.semaphore_signal(
            barrier, inc=1, device_id=(peer // n_sub, lax.rem(peer, n_sub)), device_id_type=MESH
        )

    pl.semaphore_wait(barrier, n - 1)


def spread_copy(n, n_sub, me, k, src, dst, send, recv, pick, slot):
    peer = lax.rem(me + k, n)
    return pltpu.make_async_remote_copy(
        src_ref=src.at[peer] if pick else src,
        dst_ref=dst.at[slot],
        send_sem=send.at[k],
        recv_sem=recv.at[slot],
        device_id=(peer // n_sub, lax.rem(peer, n_sub)),
        device_id_type=MESH,
    )


def first_kernel(n_dom, n_sub, hub, pay, hub_out, pay_out, s1, r1, s2, r2):
    n = n_dom * n_sub
    me = lax.axis_index("dom") * n_sub + lax.axis_index("sub")
    enter(n, n_sub, me)
    pairs = ((pay, pay_out, s2, r2, True), (hub, hub_out, s1, r1, False))

    @pl.loop(1, n)
    def _(k):
        for src, dst, send, recv, pick in pairs:
            spread_copy(n, n_sub, me, k, src, dst, send, recv, pick, me).start()

    hub_out[me] = hub[...]
    pay_out[me] = pay[me]

    @pl.loop(1, n)
    def _(k):
        peer = lax.rem(me + k, n)
        for src, dst, send, recv, pick in pairs:
            copy = spread_copy(n, n_sub, me, k, src, dst, send, recv, pick, peer)
            copy.wait_recv()
            copy.wait_send()


def last_kernel(n_dom, n_sub, pay, bias, w, pay_out, bias_out, w_out, in1, acc1, in2, acc2, in3,
                s1, r1, s2, r2, ws, wr, ys, yr, ds, dr):
    n = n_dom * n_sub
    n_y = n_sub // 2
    dom, sub = lax.axis_index("dom"), lax.axis_index("sub")
    me = dom * n_sub + sub
    y, core = sub // 2, lax.rem(sub, 2)
    enter(n, n_sub, me)
    pairs = ((pay, pay_out, s2, r2, True), (bias, bias_out, s1, r1, False))

    def core_copy(phase):
        return pltpu.make_async_remote_copy(
            src_ref=w.at[1 - core] if phase == 0 else w_out.at[core],
            dst_ref=in1 if phase == 0 else w_out.at[core],
            send_sem=ws.at[phase],
            recv_sem=wr.at[phase],
            device_id=(dom, y * 2 + 1 - core),
            device_id_type=MESH,
        )

    def y_copy(phase, k, slot):
        other = lax.rem(y + k, n_y)
        return pltpu.make_async_remote_copy(
            src_ref=acc1.at[other] if phase == 0 else w_out.at[core, y],
            dst_ref=in2.at[slot] if phase == 0 else w_out.at[core, slot],
            send_sem=ys.at[phase, k],
            recv_sem=yr.at[phase, slot],
            device_id=(dom, other * 2 + core),
            device_id_type=MESH,
        )

    def d_copy(phase, k, slot):
        other = lax.rem(dom + k, n_dom)
        return pltpu.make_async_remote_copy(
            src_ref=acc2.at[other] if phase == 0 else w_out.at[core, y, dom],
            dst_ref=in3.at[slot] if phase == 0 else w_out.at[core, y, slot],
            send_sem=ds.at[phase, k],
            recv_sem=dr.at[phase, slot],
            device_id=(other, sub),
            device_id_type=MESH,
        )

    core_copy(0).start()

    @pl.loop(1, n)
    def _(k):
        for src, dst, send, recv, pick in pairs:
            spread_copy(n, n_sub, me, k, src, dst, send, recv, pick, me).start()

    pay_out[me] = pay[me]
    bias_out[me] = bias[...]
    core_copy(0).wait()
    for q in range(n_y):

        @pl.loop(0, n_dom)
        def _(i):
            acc1[q, i] = (
                w[core, q, i].astype(jnp.float32) + in1[q, i].astype(jnp.float32)
            ).astype(acc1.dtype)

    for k in range(1, n_y):
        y_copy(0, k, y).start()
    for k in range(1, n_y):
        y_copy(0, k, lax.rem(y + k, n_y)).wait()

    @pl.loop(0, n_dom)
    def _(i):
        total = acc1[y, i].astype(jnp.float32)
        for k in range(1, n_y):
            total = total + in2[lax.rem(y + k, n_y), i].astype(jnp.float32)
        acc2[i] = total.astype(acc2.dtype)

    for k in range(1, n_dom):
        d_copy(0, k, dom).start()
    for k in range(1, n_dom):
        d_copy(0, k, lax.rem(dom + k, n_dom)).wait()
    total = acc2[dom].astype(jnp.float32)
    for k in range(1, n_dom):
        total = total + in3[lax.rem(dom + k, n_dom)].astype(jnp.float32)
    w_out[core, y, dom] = total.astype(w_out.dtype)

    for k in range(1, n_dom):
        d_copy(1, k, dom).start()
    for k in range(1, n_dom):
        d_copy(1, k, lax.rem(dom + k, n_dom)).wait()
    for k in range(1, n_y):
        y_copy(1, k, y).start()
    for k in range(1, n_y):
        y_copy(1, k, lax.rem(y + k, n_y)).wait()
    send_back = core_copy(1)
    send_back.start()

    @pl.loop(1, n)
    def _(k):
        peer = lax.rem(me + k, n)
        for src, dst, send, recv, pick in pairs:
            copy = spread_copy(n, n_sub, me, k, src, dst, send, recv, pick, peer)
            copy.wait_recv()
            copy.wait_send()

    send_back.wait_send()
    pltpu.make_async_remote_copy(
        src_ref=w_out.at[core],
        dst_ref=w_out.at[1 - core],
        send_sem=ws.at[1],
        recv_sem=wr.at[1],
        device_id=(dom, y * 2 + 1 - core),
        device_id_type=MESH,
    ).wait_recv()


VM = pl.BlockSpec(memory_space=pltpu.VMEM)
DMA = pltpu.SemaphoreType.DMA


def first_exchange(n_dom, n_sub, hub, pay):
    n = n_dom * n_sub
    return pl.pallas_call(
        functools.partial(first_kernel, n_dom, n_sub),
        out_shape=(
            jax.ShapeDtypeStruct((n,) + hub.shape, hub.dtype),
            jax.ShapeDtypeStruct(pay.shape, pay.dtype),
        ),
        in_specs=[VM, VM],
        out_specs=(VM, VM),
        scratch_shapes=[DMA((n,))] * 4,
        compiler_params=pltpu.CompilerParams(
            collective_id=0, has_side_effects=True, vmem_limit_bytes=48 * 1024 * 1024
        ),
    )(hub, pay)


def last_exchange(n_dom, n_sub, pay, bias, w):
    n = n_dom * n_sub
    tail = w.shape[3:]
    n_y = n_sub // 2
    return pl.pallas_call(
        functools.partial(last_kernel, n_dom, n_sub),
        out_shape=(
            jax.ShapeDtypeStruct(pay.shape, pay.dtype),
            jax.ShapeDtypeStruct((n,) + bias.shape, bias.dtype),
            jax.ShapeDtypeStruct(w.shape, w.dtype),
        ),
        in_specs=[VM] * 3,
        out_specs=(VM,) * 3,
        scratch_shapes=[
            pltpu.VMEM((n_y, n_dom) + tail, w.dtype),
            pltpu.VMEM((n_y, n_dom) + tail, w.dtype),
            pltpu.VMEM((n_y, n_dom) + tail, w.dtype),
            pltpu.VMEM((n_dom,) + tail, w.dtype),
            pltpu.VMEM((n_dom,) + tail, w.dtype),
            DMA((n,)), DMA((n,)), DMA((n,)), DMA((n,)),
            DMA((2,)), DMA((2,)),
            DMA((2, n_y)), DMA((2, n_y)),
            DMA((2, n_dom)), DMA((2, n_dom)),
        ],
        compiler_params=pltpu.CompilerParams(
            collective_id=1, has_side_effects=True, vmem_limit_bytes=48 * 1024 * 1024
        ),
    )(pay, bias, w)


def silu_slope(values):
    sigma = jax.nn.sigmoid(values)
    return sigma * (1.0 + values * (1.0 - sigma))


def tile_apply(source, tile_pos, live_count, tile_bits, tile_size, backward):
    n_tiles = source.shape[0] // tile_size
    slots_all = tile_bits.shape[0]
    live = (jnp.arange(slots_all) < live_count).astype(jnp.int32)
    weights_tile = (tile_bits * live[:, None, None]).astype(jnp.bfloat16)
    blocks = source.reshape(n_tiles, tile_size, -1)
    if backward:
        picked = blocks[tile_pos[:, 0]]
        product = jnp.einsum(
            "tij,tid->tjd", weights_tile, picked, preferred_element_type=jnp.float32
        )
        target = tile_pos[:, 1]
    else:
        picked = blocks[tile_pos[:, 1]]
        product = jnp.einsum(
            "tij,tjd->tid", weights_tile, picked, preferred_element_type=jnp.float32
        )
        target = tile_pos[:, 0]
    placing = (target[None, :] == jnp.arange(n_tiles)[:, None]).astype(jnp.float32)
    return jnp.einsum("kt,tid->kid", placing, product, precision=lax.Precision.HIGHEST).reshape(
        source.shape[0], -1
    )


def per_device(
    features,
    hub_features,
    w_self,
    w_neigh,
    out_bias,
    tile_index,
    tile_count,
    tile_mask,
    mirror_slot,
    mirror_edges,
    row_degree,
    hub_degree,
    grad_rows,
    grad_hubs,
):
    my_slots = mirror_slot[0]
    n_dev, n_slots = my_slots.shape
    n_hubs = hub_features.shape[0]
    tile_size = tile_mask.shape[1]
    live_slot = (my_slots >= 0).reshape(-1)
    owner_row = (
        jnp.arange(n_dev, dtype=jnp.int32)[:, None] * n_hubs + jnp.maximum(my_slots, 0)
    ).reshape(-1)
    edge_mat = (mirror_edges[0] * live_slot[:, None].astype(jnp.int32)).astype(jnp.bfloat16)
    tile_pos = tile_index[0]
    live_count = tile_count[0]

    n_sub = lax.axis_size("sub")
    n_dom = lax.axis_size("dom")
    width = features.shape[1]

    mirror_part = jnp.dot(edge_mat, features, preferred_element_type=jnp.float32)
    ids = jnp.broadcast_to(my_slots.astype(jnp.float32)[:, :, None], (n_dev, n_slots, 128))
    hubs_all, parts = first_exchange(
        n_dom,
        n_sub,
        hub_features,
        jnp.concatenate([mirror_part.reshape(n_dev, n_slots, width), ids], axis=2),
    )
    parts = parts.reshape(n_dev * n_slots, -1)
    chosen = (
        parts[:, width][None, :] == jnp.arange(n_hubs, dtype=jnp.float32)[:, None]
    ).astype(jnp.float32)
    settle = lambda rows: jnp.dot(chosen, rows, precision=lax.Precision.HIGHEST)
    picked = (owner_row[:, None] == jnp.arange(n_dev * n_hubs)[None, :]).astype(jnp.bfloat16)
    mirror_x = jnp.dot(picked, hubs_all.reshape(n_dev * n_hubs, width))
    hub_sum = settle(parts[:, :width])
    row_sum = tile_apply(features, tile_pos, live_count, tile_mask, tile_size, False) + jnp.einsum(
        "mr,md->rd", edge_mat, mirror_x, preferred_element_type=jnp.float32
    )
    degree_rows = row_degree[:, None].astype(jnp.float32)
    degree_hubs = hub_degree[:, None].astype(jnp.float32)
    mean_rows = (row_sum / degree_rows).astype(jnp.bfloat16)
    mean_hubs = (hub_sum / degree_hubs).astype(jnp.bfloat16)
    pre_rows = (
        jnp.dot(features, w_self, preferred_element_type=jnp.float32)
        + jnp.dot(mean_rows, w_neigh, preferred_element_type=jnp.float32)
        + out_bias
    )
    pre_hubs = (
        jnp.dot(hub_features, w_self, preferred_element_type=jnp.float32)
        + jnp.dot(mean_hubs, w_neigh, preferred_element_type=jnp.float32)
        + out_bias
    )
    out_rows = jax.nn.silu(pre_rows).astype(jnp.bfloat16)
    out_hubs = jax.nn.silu(pre_hubs).astype(jnp.bfloat16)
    d_pre_rows = (grad_rows.astype(jnp.float32) * silu_slope(pre_rows)).astype(jnp.bfloat16)
    d_pre_hubs = (grad_hubs.astype(jnp.float32) * silu_slope(pre_hubs)).astype(jnp.bfloat16)
    grad_self = jnp.einsum(
        "rd,rf->df", features, d_pre_rows, preferred_element_type=jnp.float32
    ) + jnp.einsum("rd,rf->df", hub_features, d_pre_hubs, preferred_element_type=jnp.float32)
    grad_neigh = jnp.einsum(
        "rd,rf->df", mean_rows, d_pre_rows, preferred_element_type=jnp.float32
    ) + jnp.einsum("rd,rf->df", mean_hubs, d_pre_hubs, preferred_element_type=jnp.float32)
    grad_bias = jnp.sum(d_pre_rows.astype(jnp.float32), axis=0) + jnp.sum(
        d_pre_hubs.astype(jnp.float32), axis=0
    )
    d_sum_rows = (
        jnp.einsum("rf,df->rd", d_pre_rows, w_neigh, preferred_element_type=jnp.float32)
        / degree_rows
    ).astype(jnp.bfloat16)
    d_sum_hubs = (
        jnp.einsum("rf,df->rd", d_pre_hubs, w_neigh, preferred_element_type=jnp.float32)
        / degree_hubs
    ).astype(jnp.bfloat16)
    mirror_back = jnp.dot(edge_mat, d_sum_rows, preferred_element_type=jnp.float32)
    sent_d = jnp.dot(
        chosen.astype(jnp.bfloat16).T, d_sum_hubs, preferred_element_type=jnp.float32
    )
    total = 2 * w_self.shape[0] * w_self.shape[1]
    block_rows = max(16, total // (w_self.shape[1] * n_dev))
    grads = jnp.concatenate([grad_self, grad_neigh], axis=0).astype(jnp.bfloat16)
    rows_back, bias_all, grads = last_exchange(
        n_dom,
        n_sub,
        jnp.concatenate(
            [mirror_back.reshape(n_dev, n_slots, width), sent_d.reshape(n_dev, n_slots, width)],
            axis=1,
        ),
        grad_bias[None, :],
        grads.reshape(2, n_sub // 2, n_dom, block_rows, total // (n_dev * block_rows)),
    )
    hub_back = settle(rows_back[:, :n_slots].reshape(n_dev * n_slots, width))
    mirror_d = rows_back[:, n_slots:].reshape(n_dev * n_slots, width).astype(jnp.bfloat16)
    grads = grads.reshape(2, *w_self.shape).astype(jnp.float32)
    d_rows = (
        jnp.einsum("rf,df->rd", d_pre_rows, w_self, preferred_element_type=jnp.float32)
        + tile_apply(d_sum_rows, tile_pos, live_count, tile_mask, tile_size, True)
        + jnp.einsum("mr,md->rd", edge_mat, mirror_d, preferred_element_type=jnp.float32)
    )
    d_hubs = (
        jnp.einsum("rf,df->rd", d_pre_hubs, w_self, preferred_element_type=jnp.float32) + hub_back
    )
    return (
        out_rows,
        out_hubs,
        d_rows.astype(jnp.bfloat16),
        d_hubs.astype(jnp.bfloat16),
        grads[0],
        grads[1],
        jnp.sum(bias_all, axis=(0, 1)),
    )


def solution(mesh):
    return jax.shard_map(
        per_device,
        mesh=mesh,
        in_specs=(
            P(("dom", "sub"), None),
            P(("dom", "sub"), None),
            P(),
            P(),
            P(),
            P(("dom", "sub"), None, None),
            P(("dom", "sub")),
            P(("dom", "sub"), None, None),
            P(("dom", "sub"), None, None),
            P(("dom", "sub"), None, None),
            P(("dom", "sub")),
            P(("dom", "sub")),
            P(("dom", "sub"), None),
            P(("dom", "sub"), None),
        ),
        out_specs=(
            P(("dom", "sub"), None),
            P(("dom", "sub"), None),
            P(("dom", "sub"), None),
            P(("dom", "sub"), None),
            P(),
            P(),
            P(),
        ),
        check_vma=False,
    )
```

```python
import functools

import jax
import jax.numpy as jnp
from jax import lax
from jax.experimental import pallas as pl
from jax.experimental.pallas import tpu as pltpu
from jax.sharding import PartitionSpec as P

MESH = pl.DeviceIdType.MESH


def enter(n, n_sub, me):
    barrier = pltpu.get_barrier_semaphore()

    @pl.loop(1, n)
    def _(k):
        peer = lax.rem(me + k, n)
        pl.semaphore_signal(
            barrier, inc=1, device_id=(peer // n_sub, lax.rem(peer, n_sub)), device_id_type=MESH
        )

    pl.semaphore_wait(barrier, n - 1)


def spread_copy(n, n_sub, me, k, src, dst, send, recv, pick, slot):
    peer = lax.rem(me + k, n)
    return pltpu.make_async_remote_copy(
        src_ref=src.at[peer] if pick else src,
        dst_ref=dst.at[slot],
        send_sem=send.at[k],
        recv_sem=recv.at[slot],
        device_id=(peer // n_sub, lax.rem(peer, n_sub)),
        device_id_type=MESH,
    )


def first_kernel(n_dom, n_sub, hub, pay, hub_out, pay_out, s1, r1, s2, r2):
    n = n_dom * n_sub
    me = lax.axis_index("dom") * n_sub + lax.axis_index("sub")
    enter(n, n_sub, me)
    pairs = ((pay, pay_out, s2, r2, True), (hub, hub_out, s1, r1, False))

    @pl.loop(1, n)
    def _(k):
        for src, dst, send, recv, pick in pairs:
            spread_copy(n, n_sub, me, k, src, dst, send, recv, pick, me).start()

    hub_out[me] = hub[...]
    pay_out[me] = pay[me]

    @pl.loop(1, n)
    def _(k):
        peer = lax.rem(me + k, n)
        for src, dst, send, recv, pick in pairs:
            copy = spread_copy(n, n_sub, me, k, src, dst, send, recv, pick, peer)
            copy.wait_recv()
            copy.wait_send()


def last_kernel(n_dom, n_sub, pay, bias, w, pay_out, bias_out, w_out, in1, acc1, in2, acc2, in3,
                s1, r1, s2, r2, ws, wr, ys, yr, ds, dr):
    n = n_dom * n_sub
    n_y = n_sub // 2
    dom, sub = lax.axis_index("dom"), lax.axis_index("sub")
    me = dom * n_sub + sub
    y, core = sub // 2, lax.rem(sub, 2)
    enter(n, n_sub, me)
    pairs = ((pay, pay_out, s2, r2, True), (bias, bias_out, s1, r1, False))

    def core_copy(phase):
        return pltpu.make_async_remote_copy(
            src_ref=w.at[1 - core] if phase == 0 else w_out.at[core],
            dst_ref=in1 if phase == 0 else w_out.at[core],
            send_sem=ws.at[phase],
            recv_sem=wr.at[phase],
            device_id=(dom, y * 2 + 1 - core),
            device_id_type=MESH,
        )

    def y_copy(phase, k, slot):
        other = lax.rem(y + k, n_y)
        return pltpu.make_async_remote_copy(
            src_ref=acc1.at[other] if phase == 0 else w_out.at[core, y],
            dst_ref=in2.at[slot] if phase == 0 else w_out.at[core, slot],
            send_sem=ys.at[phase, k],
            recv_sem=yr.at[phase, slot],
            device_id=(dom, other * 2 + core),
            device_id_type=MESH,
        )

    def d_copy(phase, k, slot):
        other = lax.rem(dom + k, n_dom)
        return pltpu.make_async_remote_copy(
            src_ref=acc2.at[other] if phase == 0 else w_out.at[core, y, dom],
            dst_ref=in3.at[slot] if phase == 0 else w_out.at[core, y, slot],
            send_sem=ds.at[phase, k],
            recv_sem=dr.at[phase, slot],
            device_id=(other, sub),
            device_id_type=MESH,
        )

    core_copy(0).start()

    @pl.loop(1, n)
    def _(k):
        for src, dst, send, recv, pick in pairs:
            spread_copy(n, n_sub, me, k, src, dst, send, recv, pick, me).start()

    pay_out[me] = pay[me]
    bias_out[me] = bias[...]
    core_copy(0).wait()
    for q in range(n_y):

        @pl.loop(0, n_dom)
        def _(i):
            acc1[q, i] = (
                w[core, q, i].astype(jnp.float32) + in1[q, i].astype(jnp.float32)
            ).astype(acc1.dtype)

    for k in range(1, n_y):
        y_copy(0, k, y).start()
    for k in range(1, n_y):
        y_copy(0, k, lax.rem(y + k, n_y)).wait()

    @pl.loop(0, n_dom)
    def _(i):
        total = acc1[y, i].astype(jnp.float32)
        for k in range(1, n_y):
            total = total + in2[lax.rem(y + k, n_y), i].astype(jnp.float32)
        acc2[i] = total.astype(acc2.dtype)

    for k in range(1, n_dom):
        d_copy(0, k, dom).start()
    for k in range(1, n_dom):
        d_copy(0, k, lax.rem(dom + k, n_dom)).wait()
    total = acc2[dom].astype(jnp.float32)
    for k in range(1, n_dom):
        total = total + in3[lax.rem(dom + k, n_dom)].astype(jnp.float32)
    w_out[core, y, dom] = total.astype(w_out.dtype)

    for k in range(1, n_dom):
        d_copy(1, k, dom).start()
    for k in range(1, n_dom):
        d_copy(1, k, lax.rem(dom + k, n_dom)).wait()
    for k in range(1, n_y):
        y_copy(1, k, y).start()
    for k in range(1, n_y):
        y_copy(1, k, lax.rem(y + k, n_y)).wait()
    send_back = core_copy(1)
    send_back.start()

    @pl.loop(1, n)
    def _(k):
        peer = lax.rem(me + k, n)
        for src, dst, send, recv, pick in pairs:
            copy = spread_copy(n, n_sub, me, k, src, dst, send, recv, pick, peer)
            copy.wait_recv()
            copy.wait_send()

    send_back.wait_send()
    pltpu.make_async_remote_copy(
        src_ref=w_out.at[core],
        dst_ref=w_out.at[1 - core],
        send_sem=ws.at[1],
        recv_sem=wr.at[1],
        device_id=(dom, y * 2 + 1 - core),
        device_id_type=MESH,
    ).wait_recv()


VM = pl.BlockSpec(memory_space=pltpu.VMEM)
DMA = pltpu.SemaphoreType.DMA


def first_exchange(n_dom, n_sub, hub, pay):
    n = n_dom * n_sub
    return pl.pallas_call(
        functools.partial(first_kernel, n_dom, n_sub),
        out_shape=(
            jax.ShapeDtypeStruct((n,) + hub.shape, hub.dtype),
            jax.ShapeDtypeStruct(pay.shape, pay.dtype),
        ),
        in_specs=[VM, VM],
        out_specs=(VM, VM),
        scratch_shapes=[DMA((n,))] * 4,
        compiler_params=pltpu.CompilerParams(
            collective_id=0, has_side_effects=True, vmem_limit_bytes=48 * 1024 * 1024
        ),
    )(hub, pay)


def last_exchange(n_dom, n_sub, pay, bias, w):
    n = n_dom * n_sub
    tail = w.shape[3:]
    n_y = n_sub // 2
    return pl.pallas_call(
        functools.partial(last_kernel, n_dom, n_sub),
        out_shape=(
            jax.ShapeDtypeStruct(pay.shape, pay.dtype),
            jax.ShapeDtypeStruct((n,) + bias.shape, bias.dtype),
            jax.ShapeDtypeStruct(w.shape, w.dtype),
        ),
        in_specs=[VM] * 3,
        out_specs=(VM,) * 3,
        scratch_shapes=[
            pltpu.VMEM((n_y, n_dom) + tail, w.dtype),
            pltpu.VMEM((n_y, n_dom) + tail, w.dtype),
            pltpu.VMEM((n_y, n_dom) + tail, w.dtype),
            pltpu.VMEM((n_dom,) + tail, w.dtype),
            pltpu.VMEM((n_dom,) + tail, w.dtype),
            DMA((n,)), DMA((n,)), DMA((n,)), DMA((n,)),
            DMA((2,)), DMA((2,)),
            DMA((2, n_y)), DMA((2, n_y)),
            DMA((2, n_dom)), DMA((2, n_dom)),
        ],
        compiler_params=pltpu.CompilerParams(
            collective_id=1, has_side_effects=True, vmem_limit_bytes=48 * 1024 * 1024
        ),
    )(pay, bias, w)


def silu_slope(values):
    sigma = jax.nn.sigmoid(values)
    return sigma * (1.0 + values * (1.0 - sigma))


def adjacency_kernel(place, count, bits, out):
    tile = bits.shape[1]

    @pl.loop(0, out.shape[0] // tile)
    def _(i):
        rows = pl.ds(pl.multiple_of(i * tile, tile), tile)
        out[rows, :] = jnp.zeros((tile, out.shape[1]), out.dtype)

    @pl.loop(0, jnp.minimum(count[0], bits.shape[0]))
    def _(t):
        rows = pl.ds(pl.multiple_of(place[2 * t] * tile, tile), tile)
        cols = pl.ds(pl.multiple_of(place[2 * t + 1] * tile, tile), tile)
        out[rows, cols] = out[rows, cols] + bits[t].astype(jnp.float32).astype(out.dtype)


def adjacency(n_rows, tile_pos, live_count, tile_bits):
    smem = pl.BlockSpec(memory_space=pltpu.SMEM)
    return pl.pallas_call(
        adjacency_kernel,
        out_shape=jax.ShapeDtypeStruct((n_rows, n_rows), jnp.bfloat16),
        in_specs=[smem, smem, VM],
        out_specs=VM,
        compiler_params=pltpu.CompilerParams(vmem_limit_bytes=48 * 1024 * 1024),
    )(tile_pos.reshape(-1), live_count, tile_bits)


def per_device(
    features,
    hub_features,
    w_self,
    w_neigh,
    out_bias,
    tile_index,
    tile_count,
    tile_mask,
    mirror_slot,
    mirror_edges,
    row_degree,
    hub_degree,
    grad_rows,
    grad_hubs,
):
    my_slots = mirror_slot[0]
    n_dev, n_slots = my_slots.shape
    n_hubs = hub_features.shape[0]
    live_slot = (my_slots >= 0).reshape(-1)
    owner_row = (
        jnp.arange(n_dev, dtype=jnp.int32)[:, None] * n_hubs + jnp.maximum(my_slots, 0)
    ).reshape(-1)
    edge_mat = (mirror_edges[0] * live_slot[:, None].astype(jnp.int32)).astype(jnp.bfloat16)
    tile_pos = tile_index[0]
    adjacent = adjacency(features.shape[0], tile_pos, tile_count, tile_mask)

    n_sub = lax.axis_size("sub")
    n_dom = lax.axis_size("dom")
    width = features.shape[1]

    mirror_part = jnp.dot(edge_mat, features, preferred_element_type=jnp.float32)
    ids = jnp.broadcast_to(my_slots.astype(jnp.float32)[:, :, None], (n_dev, n_slots, 128))
    hubs_all, parts = first_exchange(
        n_dom,
        n_sub,
        hub_features,
        jnp.concatenate([mirror_part.reshape(n_dev, n_slots, width), ids], axis=2),
    )
    parts = parts.reshape(n_dev * n_slots, -1)
    chosen = (
        parts[:, width][None, :] == jnp.arange(n_hubs, dtype=jnp.float32)[:, None]
    ).astype(jnp.float32)
    settle = lambda rows: jnp.dot(chosen, rows, precision=lax.Precision.HIGHEST)
    picked = (owner_row[:, None] == jnp.arange(n_dev * n_hubs)[None, :]).astype(jnp.bfloat16)
    mirror_x = jnp.dot(picked, hubs_all.reshape(n_dev * n_hubs, width))
    hub_sum = settle(parts[:, :width])
    row_sum = jnp.dot(adjacent, features, preferred_element_type=jnp.float32) + jnp.einsum(
        "mr,md->rd", edge_mat, mirror_x, preferred_element_type=jnp.float32
    )
    degree_rows = row_degree[:, None].astype(jnp.float32)
    degree_hubs = hub_degree[:, None].astype(jnp.float32)
    mean_rows = (row_sum / degree_rows).astype(jnp.bfloat16)
    mean_hubs = (hub_sum / degree_hubs).astype(jnp.bfloat16)
    pre_rows = (
        jnp.dot(features, w_self, preferred_element_type=jnp.float32)
        + jnp.dot(mean_rows, w_neigh, preferred_element_type=jnp.float32)
        + out_bias
    )
    pre_hubs = (
        jnp.dot(hub_features, w_self, preferred_element_type=jnp.float32)
        + jnp.dot(mean_hubs, w_neigh, preferred_element_type=jnp.float32)
        + out_bias
    )
    out_rows = jax.nn.silu(pre_rows).astype(jnp.bfloat16)
    out_hubs = jax.nn.silu(pre_hubs).astype(jnp.bfloat16)
    d_pre_rows = (grad_rows.astype(jnp.float32) * silu_slope(pre_rows)).astype(jnp.bfloat16)
    d_pre_hubs = (grad_hubs.astype(jnp.float32) * silu_slope(pre_hubs)).astype(jnp.bfloat16)
    grad_self = jnp.einsum(
        "rd,rf->df", features, d_pre_rows, preferred_element_type=jnp.float32
    ) + jnp.einsum("rd,rf->df", hub_features, d_pre_hubs, preferred_element_type=jnp.float32)
    grad_neigh = jnp.einsum(
        "rd,rf->df", mean_rows, d_pre_rows, preferred_element_type=jnp.float32
    ) + jnp.einsum("rd,rf->df", mean_hubs, d_pre_hubs, preferred_element_type=jnp.float32)
    grad_bias = jnp.sum(d_pre_rows.astype(jnp.float32), axis=0) + jnp.sum(
        d_pre_hubs.astype(jnp.float32), axis=0
    )
    d_sum_rows = (
        jnp.einsum("rf,df->rd", d_pre_rows, w_neigh, preferred_element_type=jnp.float32)
        / degree_rows
    ).astype(jnp.bfloat16)
    d_sum_hubs = (
        jnp.einsum("rf,df->rd", d_pre_hubs, w_neigh, preferred_element_type=jnp.float32)
        / degree_hubs
    ).astype(jnp.bfloat16)
    mirror_back = jnp.dot(edge_mat, d_sum_rows, preferred_element_type=jnp.float32)
    sent_d = jnp.dot(
        chosen.astype(jnp.bfloat16).T, d_sum_hubs, preferred_element_type=jnp.float32
    )
    total = 2 * w_self.shape[0] * w_self.shape[1]
    block_rows = max(16, total // (w_self.shape[1] * n_dev))
    grads = jnp.concatenate([grad_self, grad_neigh], axis=0).astype(jnp.bfloat16)
    rows_back, bias_all, grads = last_exchange(
        n_dom,
        n_sub,
        jnp.concatenate(
            [mirror_back.reshape(n_dev, n_slots, width), sent_d.reshape(n_dev, n_slots, width)],
            axis=1,
        ),
        grad_bias[None, :],
        grads.reshape(2, n_sub // 2, n_dom, block_rows, total // (n_dev * block_rows)),
    )
    hub_back = settle(rows_back[:, :n_slots].reshape(n_dev * n_slots, width))
    mirror_d = rows_back[:, n_slots:].reshape(n_dev * n_slots, width).astype(jnp.bfloat16)
    grads = grads.reshape(2, *w_self.shape).astype(jnp.float32)
    d_rows = (
        jnp.einsum("rf,df->rd", d_pre_rows, w_self, preferred_element_type=jnp.float32)
        + jnp.einsum("ij,id->jd", adjacent, d_sum_rows, preferred_element_type=jnp.float32)
        + jnp.einsum("mr,md->rd", edge_mat, mirror_d, preferred_element_type=jnp.float32)
    )
    d_hubs = (
        jnp.einsum("rf,df->rd", d_pre_hubs, w_self, preferred_element_type=jnp.float32) + hub_back
    )
    return (
        out_rows,
        out_hubs,
        d_rows.astype(jnp.bfloat16),
        d_hubs.astype(jnp.bfloat16),
        grads[0],
        grads[1],
        jnp.sum(bias_all, axis=(0, 1)),
    )


def solution(mesh):
    return jax.shard_map(
        per_device,
        mesh=mesh,
        in_specs=(
            P(("dom", "sub"), None),
            P(("dom", "sub"), None),
            P(),
            P(),
            P(),
            P(("dom", "sub"), None, None),
            P(("dom", "sub")),
            P(("dom", "sub"), None, None),
            P(("dom", "sub"), None, None),
            P(("dom", "sub"), None, None),
            P(("dom", "sub")),
            P(("dom", "sub")),
            P(("dom", "sub"), None),
            P(("dom", "sub"), None),
        ),
        out_specs=(
            P(("dom", "sub"), None),
            P(("dom", "sub"), None),
            P(("dom", "sub"), None),
            P(("dom", "sub"), None),
            P(),
            P(),
            P(),
        ),
        check_vma=False,
    )
```

```python
import functools

import jax
import jax.numpy as jnp
from jax import lax
from jax.experimental import pallas as pl
from jax.experimental.pallas import tpu as pltpu
from jax.sharding import PartitionSpec as P

MESH = pl.DeviceIdType.MESH


def enter(n, n_sub, me):
    barrier = pltpu.get_barrier_semaphore()

    @pl.loop(1, n)
    def _(k):
        peer = lax.rem(me + k, n)
        pl.semaphore_signal(
            barrier, inc=1, device_id=(peer // n_sub, lax.rem(peer, n_sub)), device_id_type=MESH
        )

    pl.semaphore_wait(barrier, n - 1)


def spread_copy(n, n_sub, me, k, src, dst, send, recv, pick, slot):
    peer = lax.rem(me + k, n)
    return pltpu.make_async_remote_copy(
        src_ref=src.at[peer] if pick else src,
        dst_ref=dst.at[slot],
        send_sem=send.at[k],
        recv_sem=recv.at[slot],
        device_id=(peer // n_sub, lax.rem(peer, n_sub)),
        device_id_type=MESH,
    )


def tile_sums(adjacent, source, out, backward, first, last):
    step = min(256, out.shape[0])
    n_steps = out.shape[0] // step

    @pl.loop(n_steps * first // 8, n_steps * last // 8)
    def _(i):
        block = pl.ds(pl.multiple_of(i * step, step), step)
        if backward:
            out[block, :] = lax.dot_general(
                adjacent[:, block],
                source[...],
                (((0,), (0,)), ((), ())),
                preferred_element_type=jnp.float32,
            )
        else:
            out[block, :] = jnp.dot(
                adjacent[block, :], source[...], preferred_element_type=jnp.float32
            )


def first_kernel(n_dom, n_sub, hub, pay, adjacent, source, hub_out, pay_out, sums, s1, r1, s2, r2):
    n = n_dom * n_sub
    me = lax.axis_index("dom") * n_sub + lax.axis_index("sub")
    enter(n, n_sub, me)
    pairs = ((pay, pay_out, s2, r2, True), (hub, hub_out, s1, r1, False))

    @pl.loop(1, n)
    def _(k):
        for src, dst, send, recv, pick in pairs:
            spread_copy(n, n_sub, me, k, src, dst, send, recv, pick, me).start()

    hub_out[me] = hub[...]
    pay_out[me] = pay[me]
    tile_sums(adjacent, source, sums, False, 0, 8)

    @pl.loop(1, n)
    def _(k):
        peer = lax.rem(me + k, n)
        for src, dst, send, recv, pick in pairs:
            copy = spread_copy(n, n_sub, me, k, src, dst, send, recv, pick, peer)
            copy.wait_recv()
            copy.wait_send()


def last_kernel(n_dom, n_sub, pay, bias, w, adjacent, source, pay_out, bias_out, w_out, sums,
                in1, acc1, in2, acc2, in3, s1, r1, s2, r2, ws, wr, ys, yr, ds, dr):
    n = n_dom * n_sub
    n_y = n_sub // 2
    dom, sub = lax.axis_index("dom"), lax.axis_index("sub")
    me = dom * n_sub + sub
    y, core = sub // 2, lax.rem(sub, 2)
    enter(n, n_sub, me)
    pairs = ((pay, pay_out, s2, r2, True), (bias, bias_out, s1, r1, False))

    def core_copy(phase):
        return pltpu.make_async_remote_copy(
            src_ref=w.at[1 - core] if phase == 0 else w_out.at[core],
            dst_ref=in1 if phase == 0 else w_out.at[core],
            send_sem=ws.at[phase],
            recv_sem=wr.at[phase],
            device_id=(dom, y * 2 + 1 - core),
            device_id_type=MESH,
        )

    def y_copy(phase, k, slot):
        other = lax.rem(y + k, n_y)
        return pltpu.make_async_remote_copy(
            src_ref=acc1.at[other] if phase == 0 else w_out.at[core, y],
            dst_ref=in2.at[slot] if phase == 0 else w_out.at[core, slot],
            send_sem=ys.at[phase, k],
            recv_sem=yr.at[phase, slot],
            device_id=(dom, other * 2 + core),
            device_id_type=MESH,
        )

    def d_copy(phase, k, slot):
        other = lax.rem(dom + k, n_dom)
        return pltpu.make_async_remote_copy(
            src_ref=acc2.at[other] if phase == 0 else w_out.at[core, y, dom],
            dst_ref=in3.at[slot] if phase == 0 else w_out.at[core, y, slot],
            send_sem=ds.at[phase, k],
            recv_sem=dr.at[phase, slot],
            device_id=(other, sub),
            device_id_type=MESH,
        )

    core_copy(0).start()

    @pl.loop(1, n)
    def _(k):
        for src, dst, send, recv, pick in pairs:
            spread_copy(n, n_sub, me, k, src, dst, send, recv, pick, me).start()

    pay_out[me] = pay[me]
    bias_out[me] = bias[...]
    tile_sums(adjacent, source, sums, True, 0, 2)
    core_copy(0).wait()
    for q in range(n_y):

        @pl.loop(0, n_dom)
        def _(i):
            acc1[q, i] = (
                w[core, q, i].astype(jnp.float32) + in1[q, i].astype(jnp.float32)
            ).astype(acc1.dtype)

    for k in range(1, n_y):
        y_copy(0, k, y).start()
    tile_sums(adjacent, source, sums, True, 2, 4)
    for k in range(1, n_y):
        y_copy(0, k, lax.rem(y + k, n_y)).wait()

    @pl.loop(0, n_dom)
    def _(i):
        total = acc1[y, i].astype(jnp.float32)
        for k in range(1, n_y):
            total = total + in2[lax.rem(y + k, n_y), i].astype(jnp.float32)
        acc2[i] = total.astype(acc2.dtype)

    for k in range(1, n_dom):
        d_copy(0, k, dom).start()
    tile_sums(adjacent, source, sums, True, 4, 6)
    for k in range(1, n_dom):
        d_copy(0, k, lax.rem(dom + k, n_dom)).wait()
    total = acc2[dom].astype(jnp.float32)
    for k in range(1, n_dom):
        total = total + in3[lax.rem(dom + k, n_dom)].astype(jnp.float32)
    w_out[core, y, dom] = total.astype(w_out.dtype)

    for k in range(1, n_dom):
        d_copy(1, k, dom).start()
    tile_sums(adjacent, source, sums, True, 6, 8)
    for k in range(1, n_dom):
        d_copy(1, k, lax.rem(dom + k, n_dom)).wait()
    for k in range(1, n_y):
        y_copy(1, k, y).start()
    for k in range(1, n_y):
        y_copy(1, k, lax.rem(y + k, n_y)).wait()
    send_back = core_copy(1)
    send_back.start()

    @pl.loop(1, n)
    def _(k):
        peer = lax.rem(me + k, n)
        for src, dst, send, recv, pick in pairs:
            copy = spread_copy(n, n_sub, me, k, src, dst, send, recv, pick, peer)
            copy.wait_recv()
            copy.wait_send()

    send_back.wait_send()
    pltpu.make_async_remote_copy(
        src_ref=w_out.at[core],
        dst_ref=w_out.at[1 - core],
        send_sem=ws.at[1],
        recv_sem=wr.at[1],
        device_id=(dom, y * 2 + 1 - core),
        device_id_type=MESH,
    ).wait_recv()


VM = pl.BlockSpec(memory_space=pltpu.VMEM)
DMA = pltpu.SemaphoreType.DMA


def first_exchange(n_dom, n_sub, hub, pay, adjacent, source):
    n = n_dom * n_sub
    return pl.pallas_call(
        functools.partial(first_kernel, n_dom, n_sub),
        out_shape=(
            jax.ShapeDtypeStruct((n,) + hub.shape, hub.dtype),
            jax.ShapeDtypeStruct(pay.shape, pay.dtype),
            jax.ShapeDtypeStruct(source.shape, jnp.float32),
        ),
        in_specs=[VM] * 4,
        out_specs=(VM,) * 3,
        scratch_shapes=[DMA((n,))] * 4,
        compiler_params=pltpu.CompilerParams(
            collective_id=0, has_side_effects=True, vmem_limit_bytes=32 * 1024 * 1024
        ),
    )(hub, pay, adjacent, source)


def last_exchange(n_dom, n_sub, pay, bias, w, adjacent, source):
    n = n_dom * n_sub
    tail = w.shape[3:]
    n_y = n_sub // 2
    return pl.pallas_call(
        functools.partial(last_kernel, n_dom, n_sub),
        out_shape=(
            jax.ShapeDtypeStruct(pay.shape, pay.dtype),
            jax.ShapeDtypeStruct((n,) + bias.shape, bias.dtype),
            jax.ShapeDtypeStruct(w.shape, w.dtype),
            jax.ShapeDtypeStruct(source.shape, jnp.float32),
        ),
        in_specs=[VM] * 5,
        out_specs=(VM,) * 4,
        scratch_shapes=[
            pltpu.VMEM((n_y, n_dom) + tail, w.dtype),
            pltpu.VMEM((n_y, n_dom) + tail, w.dtype),
            pltpu.VMEM((n_y, n_dom) + tail, w.dtype),
            pltpu.VMEM((n_dom,) + tail, w.dtype),
            pltpu.VMEM((n_dom,) + tail, w.dtype),
            DMA((n,)), DMA((n,)), DMA((n,)), DMA((n,)),
            DMA((2,)), DMA((2,)),
            DMA((2, n_y)), DMA((2, n_y)),
            DMA((2, n_dom)), DMA((2, n_dom)),
        ],
        compiler_params=pltpu.CompilerParams(
            collective_id=1, has_side_effects=True, vmem_limit_bytes=32 * 1024 * 1024
        ),
    )(pay, bias, w, adjacent, source)


def silu_slope(values):
    sigma = jax.nn.sigmoid(values)
    return sigma * (1.0 + values * (1.0 - sigma))


def adjacency_kernel(place, count, bits, out):
    tile = bits.shape[1]

    @pl.loop(0, out.shape[0] // tile)
    def _(i):
        rows = pl.ds(pl.multiple_of(i * tile, tile), tile)
        out[rows, :] = jnp.zeros((tile, out.shape[1]), out.dtype)

    @pl.loop(0, jnp.minimum(count[0], bits.shape[0]))
    def _(t):
        rows = pl.ds(pl.multiple_of(place[2 * t] * tile, tile), tile)
        cols = pl.ds(pl.multiple_of(place[2 * t + 1] * tile, tile), tile)
        out[rows, cols] = out[rows, cols] + bits[t].astype(jnp.float32).astype(out.dtype)


def adjacency(n_rows, tile_pos, live_count, tile_bits):
    smem = pl.BlockSpec(memory_space=pltpu.SMEM)
    return pl.pallas_call(
        adjacency_kernel,
        out_shape=jax.ShapeDtypeStruct((n_rows, n_rows), jnp.bfloat16),
        in_specs=[smem, smem, VM],
        out_specs=VM,
        compiler_params=pltpu.CompilerParams(vmem_limit_bytes=32 * 1024 * 1024),
    )(tile_pos.reshape(-1), live_count, tile_bits)


def per_device(
    features,
    hub_features,
    w_self,
    w_neigh,
    out_bias,
    tile_index,
    tile_count,
    tile_mask,
    mirror_slot,
    mirror_edges,
    row_degree,
    hub_degree,
    grad_rows,
    grad_hubs,
):
    my_slots = mirror_slot[0]
    n_dev, n_slots = my_slots.shape
    n_hubs = hub_features.shape[0]
    live_slot = (my_slots >= 0).reshape(-1)
    owner_row = (
        jnp.arange(n_dev, dtype=jnp.int32)[:, None] * n_hubs + jnp.maximum(my_slots, 0)
    ).reshape(-1)
    edge_mat = (mirror_edges[0] * live_slot[:, None].astype(jnp.int32)).astype(jnp.bfloat16)
    tile_pos = tile_index[0]
    adjacent = adjacency(features.shape[0], tile_pos, tile_count, tile_mask)

    n_sub = lax.axis_size("sub")
    n_dom = lax.axis_size("dom")
    width = features.shape[1]

    mirror_part = jnp.dot(edge_mat, features, preferred_element_type=jnp.float32)
    ids = jnp.broadcast_to(my_slots.astype(jnp.float32)[:, :, None], (n_dev, n_slots, 128))
    hubs_all, parts, local_sum = first_exchange(
        n_dom,
        n_sub,
        hub_features,
        jnp.concatenate([mirror_part.reshape(n_dev, n_slots, width), ids], axis=2),
        adjacent,
        features,
    )
    parts = parts.reshape(n_dev * n_slots, -1)
    chosen = (
        parts[:, width][None, :] == jnp.arange(n_hubs, dtype=jnp.float32)[:, None]
    ).astype(jnp.float32)
    settle = lambda rows: jnp.dot(chosen, rows, precision=lax.Precision.HIGHEST)
    picked = (owner_row[:, None] == jnp.arange(n_dev * n_hubs)[None, :]).astype(jnp.bfloat16)
    mirror_x = jnp.dot(picked, hubs_all.reshape(n_dev * n_hubs, width))
    hub_sum = settle(parts[:, :width])
    row_sum = local_sum + jnp.einsum(
        "mr,md->rd", edge_mat, mirror_x, preferred_element_type=jnp.float32
    )
    degree_rows = row_degree[:, None].astype(jnp.float32)
    degree_hubs = hub_degree[:, None].astype(jnp.float32)
    mean_rows = (row_sum / degree_rows).astype(jnp.bfloat16)
    mean_hubs = (hub_sum / degree_hubs).astype(jnp.bfloat16)
    pre_rows = (
        jnp.dot(features, w_self, preferred_element_type=jnp.float32)
        + jnp.dot(mean_rows, w_neigh, preferred_element_type=jnp.float32)
        + out_bias
    )
    pre_hubs = (
        jnp.dot(hub_features, w_self, preferred_element_type=jnp.float32)
        + jnp.dot(mean_hubs, w_neigh, preferred_element_type=jnp.float32)
        + out_bias
    )
    out_rows = jax.nn.silu(pre_rows).astype(jnp.bfloat16)
    out_hubs = jax.nn.silu(pre_hubs).astype(jnp.bfloat16)
    d_pre_rows = (grad_rows.astype(jnp.float32) * silu_slope(pre_rows)).astype(jnp.bfloat16)
    d_pre_hubs = (grad_hubs.astype(jnp.float32) * silu_slope(pre_hubs)).astype(jnp.bfloat16)
    grad_self = jnp.einsum(
        "rd,rf->df", features, d_pre_rows, preferred_element_type=jnp.float32
    ) + jnp.einsum("rd,rf->df", hub_features, d_pre_hubs, preferred_element_type=jnp.float32)
    grad_neigh = jnp.einsum(
        "rd,rf->df", mean_rows, d_pre_rows, preferred_element_type=jnp.float32
    ) + jnp.einsum("rd,rf->df", mean_hubs, d_pre_hubs, preferred_element_type=jnp.float32)
    grad_bias = jnp.sum(d_pre_rows.astype(jnp.float32), axis=0) + jnp.sum(
        d_pre_hubs.astype(jnp.float32), axis=0
    )
    d_sum_rows = (
        jnp.einsum("rf,df->rd", d_pre_rows, w_neigh, preferred_element_type=jnp.float32)
        / degree_rows
    ).astype(jnp.bfloat16)
    d_sum_hubs = (
        jnp.einsum("rf,df->rd", d_pre_hubs, w_neigh, preferred_element_type=jnp.float32)
        / degree_hubs
    ).astype(jnp.bfloat16)
    mirror_back = jnp.dot(edge_mat, d_sum_rows, preferred_element_type=jnp.float32)
    sent_d = jnp.dot(
        chosen.astype(jnp.bfloat16).T, d_sum_hubs, preferred_element_type=jnp.float32
    )
    total = 2 * w_self.shape[0] * w_self.shape[1]
    block_rows = max(16, total // (w_self.shape[1] * n_dev))
    grads = jnp.concatenate([grad_self, grad_neigh], axis=0).astype(jnp.bfloat16)
    rows_back, bias_all, grads, back_sum = last_exchange(
        n_dom,
        n_sub,
        jnp.concatenate(
            [mirror_back.reshape(n_dev, n_slots, width), sent_d.reshape(n_dev, n_slots, width)],
            axis=1,
        ),
        grad_bias[None, :],
        grads.reshape(2, n_sub // 2, n_dom, block_rows, total // (n_dev * block_rows)),
        adjacent,
        d_sum_rows,
    )
    hub_back = settle(rows_back[:, :n_slots].reshape(n_dev * n_slots, width))
    mirror_d = rows_back[:, n_slots:].reshape(n_dev * n_slots, width).astype(jnp.bfloat16)
    grads = grads.reshape(2, *w_self.shape).astype(jnp.float32)
    d_rows = (
        jnp.einsum("rf,df->rd", d_pre_rows, w_self, preferred_element_type=jnp.float32)
        + back_sum
        + jnp.einsum("mr,md->rd", edge_mat, mirror_d, preferred_element_type=jnp.float32)
    )
    d_hubs = (
        jnp.einsum("rf,df->rd", d_pre_hubs, w_self, preferred_element_type=jnp.float32) + hub_back
    )
    return (
        out_rows,
        out_hubs,
        d_rows.astype(jnp.bfloat16),
        d_hubs.astype(jnp.bfloat16),
        grads[0],
        grads[1],
        jnp.sum(bias_all, axis=(0, 1)),
    )


def solution(mesh):
    return jax.shard_map(
        per_device,
        mesh=mesh,
        in_specs=(
            P(("dom", "sub"), None),
            P(("dom", "sub"), None),
            P(),
            P(),
            P(),
            P(("dom", "sub"), None, None),
            P(("dom", "sub")),
            P(("dom", "sub"), None, None),
            P(("dom", "sub"), None, None),
            P(("dom", "sub"), None, None),
            P(("dom", "sub")),
            P(("dom", "sub")),
            P(("dom", "sub"), None),
            P(("dom", "sub"), None),
        ),
        out_specs=(
            P(("dom", "sub"), None),
            P(("dom", "sub"), None),
            P(("dom", "sub"), None),
            P(("dom", "sub"), None),
            P(),
            P(),
            P(),
        ),
        check_vma=False,
    )
```

```python
import functools

import jax
import jax.numpy as jnp
from jax import lax
from jax.experimental import pallas as pl
from jax.experimental.pallas import tpu as pltpu
from jax.sharding import PartitionSpec as P

MESH = pl.DeviceIdType.MESH


def enter(n, n_sub, me):
    barrier = pltpu.get_barrier_semaphore()

    @pl.loop(1, n)
    def _(k):
        peer = lax.rem(me + k, n)
        pl.semaphore_signal(
            barrier, inc=1, device_id=(peer // n_sub, lax.rem(peer, n_sub)), device_id_type=MESH
        )

    pl.semaphore_wait(barrier, n - 1)


def spread_copy(n, n_sub, me, k, src, dst, send, recv, pick, slot):
    peer = lax.rem(me + k, n)
    return pltpu.make_async_remote_copy(
        src_ref=src.at[peer] if pick else src,
        dst_ref=dst.at[slot],
        send_sem=send.at[k],
        recv_sem=recv.at[slot],
        device_id=(peer // n_sub, lax.rem(peer, n_sub)),
        device_id_type=MESH,
    )


def tile_sums(adjacent, source, out, backward, first, last):
    step = min(256, out.shape[0])
    n_steps = out.shape[0] // step

    @pl.loop(n_steps * first // 8, n_steps * last // 8)
    def _(i):
        block = pl.ds(pl.multiple_of(i * step, step), step)
        if backward:
            out[block, :] = lax.dot_general(
                adjacent[:, block],
                source[...],
                (((0,), (0,)), ((), ())),
                preferred_element_type=jnp.float32,
            )
        else:
            out[block, :] = jnp.dot(
                adjacent[block, :], source[...], preferred_element_type=jnp.float32
            )


def first_kernel(n_dom, n_sub, hub, pay, adjacent, source, hub_out, pay_out, sums, s1, r1, s2, r2):
    n = n_dom * n_sub
    me = lax.axis_index("dom") * n_sub + lax.axis_index("sub")
    enter(n, n_sub, me)
    core, pair = lax.rem(me, 2), me // 2
    sibling = me + 1 - 2 * core

    def hub_copy(k, slot):
        peer = lax.rem(me + 2 * k, n)
        return pltpu.make_async_remote_copy(
            src_ref=hub,
            dst_ref=hub_out.at[core, slot],
            send_sem=s1.at[k],
            recv_sem=r1.at[slot],
            device_id=(peer // n_sub, lax.rem(peer, n_sub)),
            device_id_type=MESH,
        )

    def sibling_copy(half):
        return pltpu.make_async_remote_copy(
            src_ref=hub_out.at[core],
            dst_ref=hub_out.at[half],
            send_sem=s1.at[0],
            recv_sem=r1.at[n // 2],
            device_id=(sibling // n_sub, lax.rem(sibling, n_sub)),
            device_id_type=MESH,
        )

    @pl.loop(1, n // 2)
    def _(k):
        hub_copy(k, pair).start()

    @pl.loop(1, n)
    def _(k):
        spread_copy(n, n_sub, me, k, pay, pay_out, s2, r2, True, me).start()

    hub_out[core, pair] = hub[...]
    pay_out[me] = pay[me]
    tile_sums(adjacent, source, sums, False, 0, 8)

    @pl.loop(1, n // 2)
    def _(k):
        copy = hub_copy(k, lax.rem(pair + k, n // 2))
        copy.wait_recv()
        copy.wait_send()

    sibling_copy(core).start()

    @pl.loop(1, n)
    def _(k):
        copy = spread_copy(n, n_sub, me, k, pay, pay_out, s2, r2, True, lax.rem(me + k, n))
        copy.wait_recv()
        copy.wait_send()

    sibling_copy(core).wait_send()
    sibling_copy(1 - core).wait_recv()


def last_kernel(n_dom, n_sub, pay, bias, w, adjacent, source, pay_out, bias_out, w_out, sums,
                in1, acc1, in2, acc2, in3, s1, r1, s2, r2, ws, wr, ys, yr, ds, dr):
    n = n_dom * n_sub
    n_y = n_sub // 2
    dom, sub = lax.axis_index("dom"), lax.axis_index("sub")
    me = dom * n_sub + sub
    y, core = sub // 2, lax.rem(sub, 2)
    enter(n, n_sub, me)
    pairs = ((pay, pay_out, s2, r2, True), (bias, bias_out, s1, r1, False))

    def core_copy(phase):
        return pltpu.make_async_remote_copy(
            src_ref=w.at[1 - core] if phase == 0 else w_out.at[core],
            dst_ref=in1 if phase == 0 else w_out.at[core],
            send_sem=ws.at[phase],
            recv_sem=wr.at[phase],
            device_id=(dom, y * 2 + 1 - core),
            device_id_type=MESH,
        )

    def y_copy(phase, k, slot):
        other = lax.rem(y + k, n_y)
        return pltpu.make_async_remote_copy(
            src_ref=acc1.at[other] if phase == 0 else w_out.at[core, y],
            dst_ref=in2.at[slot] if phase == 0 else w_out.at[core, slot],
            send_sem=ys.at[phase, k],
            recv_sem=yr.at[phase, slot],
            device_id=(dom, other * 2 + core),
            device_id_type=MESH,
        )

    def d_copy(phase, k, slot):
        other = lax.rem(dom + k, n_dom)
        return pltpu.make_async_remote_copy(
            src_ref=acc2.at[other] if phase == 0 else w_out.at[core, y, dom],
            dst_ref=in3.at[slot] if phase == 0 else w_out.at[core, y, slot],
            send_sem=ds.at[phase, k],
            recv_sem=dr.at[phase, slot],
            device_id=(other, sub),
            device_id_type=MESH,
        )

    core_copy(0).start()

    @pl.loop(1, n)
    def _(k):
        for src, dst, send, recv, pick in pairs:
            spread_copy(n, n_sub, me, k, src, dst, send, recv, pick, me).start()

    pay_out[me] = pay[me]
    bias_out[me] = bias[...]
    tile_sums(adjacent, source, sums, True, 0, 2)
    core_copy(0).wait()
    for q in range(n_y):

        @pl.loop(0, n_dom)
        def _(i):
            acc1[q, i] = (
                w[core, q, i].astype(jnp.float32) + in1[q, i].astype(jnp.float32)
            ).astype(acc1.dtype)

    for k in range(1, n_y):
        y_copy(0, k, y).start()
    tile_sums(adjacent, source, sums, True, 2, 4)
    for k in range(1, n_y):
        y_copy(0, k, lax.rem(y + k, n_y)).wait()

    @pl.loop(0, n_dom)
    def _(i):
        total = acc1[y, i].astype(jnp.float32)
        for k in range(1, n_y):
            total = total + in2[lax.rem(y + k, n_y), i].astype(jnp.float32)
        acc2[i] = total.astype(acc2.dtype)

    for k in range(1, n_dom):
        d_copy(0, k, dom).start()
    tile_sums(adjacent, source, sums, True, 4, 6)
    for k in range(1, n_dom):
        d_copy(0, k, lax.rem(dom + k, n_dom)).wait()
    total = acc2[dom].astype(jnp.float32)
    for k in range(1, n_dom):
        total = total + in3[lax.rem(dom + k, n_dom)].astype(jnp.float32)
    w_out[core, y, dom] = total.astype(w_out.dtype)

    for k in range(1, n_dom):
        d_copy(1, k, dom).start()
    tile_sums(adjacent, source, sums, True, 6, 8)
    for k in range(1, n_dom):
        d_copy(1, k, lax.rem(dom + k, n_dom)).wait()
    for k in range(1, n_y):
        y_copy(1, k, y).start()
    for k in range(1, n_y):
        y_copy(1, k, lax.rem(y + k, n_y)).wait()
    send_back = core_copy(1)
    send_back.start()

    @pl.loop(1, n)
    def _(k):
        peer = lax.rem(me + k, n)
        for src, dst, send, recv, pick in pairs:
            copy = spread_copy(n, n_sub, me, k, src, dst, send, recv, pick, peer)
            copy.wait_recv()
            copy.wait_send()

    send_back.wait_send()
    pltpu.make_async_remote_copy(
        src_ref=w_out.at[core],
        dst_ref=w_out.at[1 - core],
        send_sem=ws.at[1],
        recv_sem=wr.at[1],
        device_id=(dom, y * 2 + 1 - core),
        device_id_type=MESH,
    ).wait_recv()


VM = pl.BlockSpec(memory_space=pltpu.VMEM)
DMA = pltpu.SemaphoreType.DMA


def first_exchange(n_dom, n_sub, hub, pay, adjacent, source):
    n = n_dom * n_sub
    return pl.pallas_call(
        functools.partial(first_kernel, n_dom, n_sub),
        out_shape=(
            jax.ShapeDtypeStruct((2, n // 2) + hub.shape, hub.dtype),
            jax.ShapeDtypeStruct(pay.shape, pay.dtype),
            jax.ShapeDtypeStruct(source.shape, jnp.float32),
        ),
        in_specs=[VM] * 4,
        out_specs=(VM,) * 3,
        scratch_shapes=[DMA((n,))] * 4,
        compiler_params=pltpu.CompilerParams(
            collective_id=0, has_side_effects=True, vmem_limit_bytes=32 * 1024 * 1024
        ),
    )(hub, pay, adjacent, source)


def last_exchange(n_dom, n_sub, pay, bias, w, adjacent, source):
    n = n_dom * n_sub
    tail = w.shape[3:]
    n_y = n_sub // 2
    return pl.pallas_call(
        functools.partial(last_kernel, n_dom, n_sub),
        out_shape=(
            jax.ShapeDtypeStruct(pay.shape, pay.dtype),
            jax.ShapeDtypeStruct((n,) + bias.shape, bias.dtype),
            jax.ShapeDtypeStruct(w.shape, w.dtype),
            jax.ShapeDtypeStruct(source.shape, jnp.float32),
        ),
        in_specs=[VM] * 5,
        out_specs=(VM,) * 4,
        scratch_shapes=[
            pltpu.VMEM((n_y, n_dom) + tail, w.dtype),
            pltpu.VMEM((n_y, n_dom) + tail, w.dtype),
            pltpu.VMEM((n_y, n_dom) + tail, w.dtype),
            pltpu.VMEM((n_dom,) + tail, w.dtype),
            pltpu.VMEM((n_dom,) + tail, w.dtype),
            DMA((n,)), DMA((n,)), DMA((n,)), DMA((n,)),
            DMA((2,)), DMA((2,)),
            DMA((2, n_y)), DMA((2, n_y)),
            DMA((2, n_dom)), DMA((2, n_dom)),
        ],
        compiler_params=pltpu.CompilerParams(
            collective_id=1, has_side_effects=True, vmem_limit_bytes=32 * 1024 * 1024
        ),
    )(pay, bias, w, adjacent, source)


def silu_slope(values):
    sigma = jax.nn.sigmoid(values)
    return sigma * (1.0 + values * (1.0 - sigma))


def adjacency_kernel(place, count, bits, out):
    tile = bits.shape[1]

    @pl.loop(0, out.shape[0] // tile)
    def _(i):
        rows = pl.ds(pl.multiple_of(i * tile, tile), tile)
        out[rows, :] = jnp.zeros((tile, out.shape[1]), out.dtype)

    @pl.loop(0, jnp.minimum(count[0], bits.shape[0]))
    def _(t):
        rows = pl.ds(pl.multiple_of(place[2 * t] * tile, tile), tile)
        cols = pl.ds(pl.multiple_of(place[2 * t + 1] * tile, tile), tile)
        out[rows, cols] = out[rows, cols] + bits[t].astype(jnp.float32).astype(out.dtype)


def adjacency(n_rows, tile_pos, live_count, tile_bits):
    smem = pl.BlockSpec(memory_space=pltpu.SMEM)
    return pl.pallas_call(
        adjacency_kernel,
        out_shape=jax.ShapeDtypeStruct((n_rows, n_rows), jnp.bfloat16),
        in_specs=[smem, smem, VM],
        out_specs=VM,
        compiler_params=pltpu.CompilerParams(vmem_limit_bytes=32 * 1024 * 1024),
    )(tile_pos.reshape(-1), live_count, tile_bits)


def per_device(
    features,
    hub_features,
    w_self,
    w_neigh,
    out_bias,
    tile_index,
    tile_count,
    tile_mask,
    mirror_slot,
    mirror_edges,
    row_degree,
    hub_degree,
    grad_rows,
    grad_hubs,
):
    my_slots = mirror_slot[0]
    n_dev, n_slots = my_slots.shape
    n_hubs = hub_features.shape[0]
    live_slot = (my_slots >= 0).reshape(-1)
    owner = jnp.arange(n_dev, dtype=jnp.int32)
    owner_row = (
        (owner % 2 * (n_dev // 2) + owner // 2)[:, None] * n_hubs + jnp.maximum(my_slots, 0)
    ).reshape(-1)
    edge_mat = (mirror_edges[0] * live_slot[:, None].astype(jnp.int32)).astype(jnp.bfloat16)
    tile_pos = tile_index[0]
    adjacent = adjacency(features.shape[0], tile_pos, tile_count, tile_mask)

    n_sub = lax.axis_size("sub")
    n_dom = lax.axis_size("dom")
    width = features.shape[1]

    mirror_part = jnp.dot(edge_mat, features, preferred_element_type=jnp.float32)
    ids = jnp.broadcast_to(my_slots.astype(jnp.float32)[:, :, None], (n_dev, n_slots, 128))
    hubs_all, parts, local_sum = first_exchange(
        n_dom,
        n_sub,
        hub_features,
        jnp.concatenate([mirror_part.reshape(n_dev, n_slots, width), ids], axis=2),
        adjacent,
        features,
    )
    parts = parts.reshape(n_dev * n_slots, -1)
    chosen = (
        parts[:, width][None, :] == jnp.arange(n_hubs, dtype=jnp.float32)[:, None]
    ).astype(jnp.float32)
    settle = lambda rows: jnp.dot(chosen, rows, precision=lax.Precision.HIGHEST)
    picked = (owner_row[:, None] == jnp.arange(n_dev * n_hubs)[None, :]).astype(jnp.bfloat16)
    mirror_x = jnp.dot(picked, hubs_all.reshape(n_dev * n_hubs, width))
    hub_sum = settle(parts[:, :width])
    row_sum = local_sum + jnp.einsum(
        "mr,md->rd", edge_mat, mirror_x, preferred_element_type=jnp.float32
    )
    degree_rows = row_degree[:, None].astype(jnp.float32)
    degree_hubs = hub_degree[:, None].astype(jnp.float32)
    mean_rows = (row_sum / degree_rows).astype(jnp.bfloat16)
    mean_hubs = (hub_sum / degree_hubs).astype(jnp.bfloat16)
    pre_rows = (
        jnp.dot(features, w_self, preferred_element_type=jnp.float32)
        + jnp.dot(mean_rows, w_neigh, preferred_element_type=jnp.float32)
        + out_bias
    )
    pre_hubs = (
        jnp.dot(hub_features, w_self, preferred_element_type=jnp.float32)
        + jnp.dot(mean_hubs, w_neigh, preferred_element_type=jnp.float32)
        + out_bias
    )
    out_rows = jax.nn.silu(pre_rows).astype(jnp.bfloat16)
    out_hubs = jax.nn.silu(pre_hubs).astype(jnp.bfloat16)
    d_pre_rows = (grad_rows.astype(jnp.float32) * silu_slope(pre_rows)).astype(jnp.bfloat16)
    d_pre_hubs = (grad_hubs.astype(jnp.float32) * silu_slope(pre_hubs)).astype(jnp.bfloat16)
    grad_self = jnp.einsum(
        "rd,rf->df", features, d_pre_rows, preferred_element_type=jnp.float32
    ) + jnp.einsum("rd,rf->df", hub_features, d_pre_hubs, preferred_element_type=jnp.float32)
    grad_neigh = jnp.einsum(
        "rd,rf->df", mean_rows, d_pre_rows, preferred_element_type=jnp.float32
    ) + jnp.einsum("rd,rf->df", mean_hubs, d_pre_hubs, preferred_element_type=jnp.float32)
    grad_bias = jnp.sum(d_pre_rows.astype(jnp.float32), axis=0) + jnp.sum(
        d_pre_hubs.astype(jnp.float32), axis=0
    )
    d_sum_rows = (
        jnp.einsum("rf,df->rd", d_pre_rows, w_neigh, preferred_element_type=jnp.float32)
        / degree_rows
    ).astype(jnp.bfloat16)
    d_sum_hubs = (
        jnp.einsum("rf,df->rd", d_pre_hubs, w_neigh, preferred_element_type=jnp.float32)
        / degree_hubs
    ).astype(jnp.bfloat16)
    mirror_back = jnp.dot(edge_mat, d_sum_rows, preferred_element_type=jnp.float32)
    sent_d = jnp.dot(
        chosen.astype(jnp.bfloat16).T, d_sum_hubs, preferred_element_type=jnp.float32
    )
    total = 2 * w_self.shape[0] * w_self.shape[1]
    block_rows = max(16, total // (w_self.shape[1] * n_dev))
    grads = jnp.concatenate([grad_self, grad_neigh], axis=0).astype(jnp.bfloat16)
    rows_back, bias_all, grads, back_sum = last_exchange(
        n_dom,
        n_sub,
        jnp.concatenate(
            [mirror_back.reshape(n_dev, n_slots, width), sent_d.reshape(n_dev, n_slots, width)],
            axis=1,
        ),
        grad_bias[None, :],
        grads.reshape(2, n_sub // 2, n_dom, block_rows, total // (n_dev * block_rows)),
        adjacent,
        d_sum_rows,
    )
    hub_back = settle(rows_back[:, :n_slots].reshape(n_dev * n_slots, width))
    mirror_d = rows_back[:, n_slots:].reshape(n_dev * n_slots, width).astype(jnp.bfloat16)
    grads = grads.reshape(2, *w_self.shape).astype(jnp.float32)
    d_rows = (
        jnp.einsum("rf,df->rd", d_pre_rows, w_self, preferred_element_type=jnp.float32)
        + back_sum
        + jnp.einsum("mr,md->rd", edge_mat, mirror_d, preferred_element_type=jnp.float32)
    )
    d_hubs = (
        jnp.einsum("rf,df->rd", d_pre_hubs, w_self, preferred_element_type=jnp.float32) + hub_back
    )
    return (
        out_rows,
        out_hubs,
        d_rows.astype(jnp.bfloat16),
        d_hubs.astype(jnp.bfloat16),
        grads[0],
        grads[1],
        jnp.sum(bias_all, axis=(0, 1)),
    )


def solution(mesh):
    return jax.shard_map(
        per_device,
        mesh=mesh,
        in_specs=(
            P(("dom", "sub"), None),
            P(("dom", "sub"), None),
            P(),
            P(),
            P(),
            P(("dom", "sub"), None, None),
            P(("dom", "sub")),
            P(("dom", "sub"), None, None),
            P(("dom", "sub"), None, None),
            P(("dom", "sub"), None, None),
            P(("dom", "sub")),
            P(("dom", "sub")),
            P(("dom", "sub"), None),
            P(("dom", "sub"), None),
        ),
        out_specs=(
            P(("dom", "sub"), None),
            P(("dom", "sub"), None),
            P(("dom", "sub"), None),
            P(("dom", "sub"), None),
            P(),
            P(),
            P(),
        ),
        check_vma=False,
    )
```
